512 devices in a mesh: dp: 8 (over z_hi, core), seq: 64 (over x, y, z_lo).
Axes of the slice: x: 4, y: 4, z: 16 (z_hi: 4, z_lo: 4; z = z_hi * 4 + z_lo), core: 2. Of those that a mesh axis runs over, the one named last changes fastest.
Arguments:
- first_gate: bfloat16 [8, 1024, 8192], P('dp', None, 'seq'), may hold values from -6 to 6
- second_gate: bfloat16 [8, 1024, 8192], P('dp', None, 'seq'), may hold values from -6 to 6
- value_proj: bfloat16 [8, 1024, 8192], P('dp', None, 'seq'), may hold values from -6 to 6
- grad_out: bfloat16 [8, 1024, 8192], P('dp', None, 'seq'), may hold values from -120 to 120
- filter_taps: float32 [64, 8192], P('seq'), may hold values from -1.5 to 1.5
- skip_bias: float32 [1024], replicated, may hold values from -1 to 1
Outputs:
- grad_first: bfloat16 [8, 1024, 8192], P('dp', None, 'seq')
- grad_second: bfloat16 [8, 1024, 8192], P('dp', None, 'seq')
- grad_value: bfloat16 [8, 1024, 8192], P('dp', None, 'seq')
- grad_filter: float32 [64, 8192], P('seq')
- grad_bias: float32 [1024], P('seq')
The draws below stay inside these ranges and needn't reach their ends.
All inputs are finite; a program needn't handle non-finite values.
Results may differ from the reference program's by a relative error of at most 0.019.
Values may be sent and summed in bfloat16 or wider, within the bound.
No kernel may reach another device: no remote copies, remote signals or barrier semaphores. Data moves between devices by JAX's collectives and lax.ppermute only.
A program may use at most 64 MiB of HBM per device.

```python
import jax
import jax.numpy as jnp
from jax import lax

C = 1024
GS = 16
FILTER_GROUPS = 64
SEQUENCE_LENGTH = 8192
SEQS = 8


def draw_grad_out(key, part):
    key = jax.random.fold_in(key, 5)
    random_key_series = jax.random.split(key, 3)
    member = jnp.arange(SEQS, dtype=jnp.float32)[:, None, None]
    seq_tilt = 3.0 ** (member / max(SEQS - 1, 1))
    position_scale = 10.0 ** jax.random.uniform(random_key_series[1], (1, 1, SEQUENCE_LENGTH), jnp.float32)
    channel_scale = 10.0 ** (0.5 * jax.random.uniform(random_key_series[2], (1, C, 1), jnp.float32))
    baseline_jitter = jnp.clip(jax.random.normal(random_key_series[0], (SEQS, C, SEQUENCE_LENGTH), jnp.float32), -5.0, 5.0)
    return (baseline_jitter * seq_tilt * position_scale * channel_scale * 0.25).astype(jnp.bfloat16)


def draw_filter_taps(key, part):
    key = jax.random.fold_in(key, 11)
    random_key_series = jax.random.split(key, 3)
    taps = jnp.arange(SEQUENCE_LENGTH, dtype=jnp.float32)[None, :]
    filter_tap_index = jnp.arange(SEQUENCE_LENGTH, dtype=jnp.int32)[None, :]
    log_rate = jax.random.uniform(random_key_series[0], (FILTER_GROUPS, 1), jnp.float32, jnp.log(1.0 / (4.0 * SEQUENCE_LENGTH)), jnp.log(1.0 / 35.0))
    baseline_jitter = jnp.clip(jax.random.normal(random_key_series[1], (FILTER_GROUPS, SEQUENCE_LENGTH), jnp.float32), -5.0, 5.0)
    decay_rate = jnp.exp(log_rate)
    decay_profile = jnp.exp(-decay_rate * taps)
    signal_power = jnp.expm1(-2.0 * decay_rate * SEQUENCE_LENGTH) / jnp.expm1(-2.0 * decay_rate)
    spike_location = jax.random.randint(random_key_series[2], (FILTER_GROUPS, 3), 0, SEQUENCE_LENGTH)
    spike_multiplier = jnp.ones((FILTER_GROUPS, SEQUENCE_LENGTH), jnp.float32)
    for item_total in range(3):
        spike_multiplier = spike_multiplier * jnp.where(filter_tap_index >= spike_location[:, item_total:item_total + 1], 0.6, 1.0)
    return baseline_jitter * decay_profile * spike_multiplier / jnp.sqrt(signal_power)


def block_levels(rng, dims, cuts, least, top_value):
    def one(position, blocks):
        heights = jax.random.uniform(jax.random.fold_in(jax.random.fold_in(rng, 6), position), (blocks,), jnp.float32, least / len(cuts), top_value / len(cuts))
        return jnp.repeat(jnp.exp(heights), dims[position] // blocks).reshape((-1,) + (1,) * (len(dims) - position - 1))

    gain = one(*cuts[0])
    for cut in cuts[1:]:
        gain = gain * one(*cut)
    return gain


def centred(own_key, extent, spread, most, cuts=(), held_as=jnp.bfloat16):
    loudness = block_levels(own_key, extent, cuts, -0.22, 0.18) if cuts else 1.0
    values = jax.random.normal(own_key, extent, jnp.float32) * spread * loudness
    return jnp.minimum(jnp.maximum(values, -most), most).astype(held_as)


def setup_inputs(seed: int = 0) -> dict:
    splits = jax.random.split(jax.random.key(seed), 7)
    first_gate = centred(splits[0], (SEQS, C, SEQUENCE_LENGTH), 1.0, 6.0, ((0, 8), (2, 64)))
    second_gate = centred(splits[1], (SEQS, C, SEQUENCE_LENGTH), 1.0, 6.0, ((0, 8), (2, 64)))
    value_proj = centred(splits[2], (SEQS, C, SEQUENCE_LENGTH), 1.0, 6.0, ((0, 8), (2, 64)))
    grad_out = draw_grad_out(jax.random.fold_in(splits[6], 71), 0)
    filter_taps = draw_filter_taps(jax.random.fold_in(splits[6], 71), 0)
    skip_bias = jnp.clip(jax.random.uniform(splits[5], (C,), jnp.float32, -1.0, 1.0), -1.0, 1.0)
    return {"first_gate": first_gate, "second_gate": second_gate, "value_proj": value_proj, "grad_out": grad_out, "filter_taps": filter_taps, "skip_bias": skip_bias}


def rounded(left_side, right_side):
    joined = left_side.astype(jnp.float32) * right_side.astype(jnp.float32)
    return lax.optimization_barrier(joined.astype(jnp.bfloat16)).astype(jnp.float32)


def settle(values):
    return lax.optimization_barrier(values.astype(jnp.bfloat16)).astype(jnp.float32)


def reference(first_gate, second_gate, value_proj, grad_out, filter_taps, skip_bias):
    padded = 2 * SEQUENCE_LENGTH
    filter_spec = jnp.fft.rfft(filter_taps, n=padded, axis=1)
    chan_spec = jnp.repeat(filter_spec, GS, axis=0)
    scale_col = skip_bias[:, None]
    grad_filter = jnp.zeros((C // GS, SEQUENCE_LENGTH), jnp.float32)
    grad_bias = jnp.zeros((C,), jnp.float32)
    firsts = []
    seconds = []
    values_out = []
    for member in range(SEQS):
        mixed_vals = rounded(first_gate[member], value_proj[member])
        weighted = rounded(grad_out[member], second_gate[member])
        mixed_spec = jnp.fft.rfft(mixed_vals, n=padded, axis=1)
        weighted_spec = jnp.fft.rfft(weighted, n=padded, axis=1)
        conv_full = jnp.fft.irfft(chan_spec * mixed_spec, n=padded, axis=1)[:, :SEQUENCE_LENGTH]
        conv_vals = settle(conv_full + scale_col * mixed_vals)
        back_full = jnp.fft.irfft(jnp.conj(chan_spec) * weighted_spec, n=padded, axis=1)[:, :SEQUENCE_LENGTH]
        back_vals = settle(back_full + scale_col * weighted)
        seconds.append((grad_out[member].astype(jnp.float32) * conv_vals).astype(jnp.bfloat16))
        firsts.append((back_vals * value_proj[member].astype(jnp.float32)).astype(jnp.bfloat16))
        values_out.append((back_vals * first_gate[member].astype(jnp.float32)).astype(jnp.bfloat16))
        cross_spec = (jnp.conj(mixed_spec) * weighted_spec).reshape(C // GS, GS, -1).sum(axis=1)
        grad_filter = grad_filter + jnp.fft.irfft(cross_spec, n=padded, axis=1)[:, :SEQUENCE_LENGTH]
        grad_bias = grad_bias + jnp.sum(mixed_vals * weighted, axis=1)
    return (jnp.stack(firsts), jnp.stack(seconds), jnp.stack(values_out), grad_filter, grad_bias)
```

```python
import functools

import jax
import jax.numpy as jnp
from jax import lax
from jax.experimental import pallas as pl
from jax.experimental.pallas import tpu as pltpu
from jax.sharding import PartitionSpec as P

f32 = jnp.float32
bf16 = jnp.bfloat16
lanes = 128
block = 256
lag_group = 4
whole = pl.BlockSpec(memory_space=pltpu.VMEM)
params = pltpu.CompilerParams(vmem_limit_bytes=40 << 20)


def times(left, right):
    return (left.astype(f32) * right.astype(f32)).astype(bf16)


def gate_kernel(first_ref, second_ref, value_ref, grad_ref, out_ref):
    chans = first_ref.shape[1]
    out_ref[:, :chans] = times(first_ref[...], value_ref[...])
    out_ref[:, chans:] = times(grad_ref[...], second_ref[...])


def gate(first, second, value, grad):
    parts, chans, width = first.shape
    step = parts // 4
    spec = pl.BlockSpec((step, chans, width), lambda i: (i, 0, 0))
    return pl.pallas_call(
        gate_kernel,
        grid=(parts // step,),
        out_shape=jax.ShapeDtypeStruct((parts, 2 * chans, width), bf16),
        in_specs=[spec] * 4,
        out_specs=pl.BlockSpec((step, 2 * chans, width), lambda i: (i, 0, 0)),
        name="gate",
    )(first, second, value, grad)


def toeplitz_kernel(taps_ref, out_ref):
    length = taps_ref.shape[1]
    zero = jnp.zeros((1, lanes), f32)
    padded = jnp.concatenate([zero, taps_ref[...]], axis=1)
    rows = jnp.broadcast_to(padded, (8, length + lanes))
    rows = pltpu.roll(rows, 0, 1, stride=1, stride_axis=0)
    for top in range(0, lanes, 16):
        upper = rows if top == 0 else pltpu.roll(rows, top, 1)
        lower = pltpu.roll(rows, top + 8, 1)
        both = jnp.concatenate([upper, lower], axis=0)
        out_ref[top : top + 16, :] = both.astype(bf16)
    out_ref[:, :lanes] = jnp.zeros((lanes, lanes), bf16)


def toeplitz(taps):
    return pl.pallas_call(
        toeplitz_kernel,
        out_shape=jax.ShapeDtypeStruct((lanes, taps.shape[1] + lanes), bf16),
        in_specs=[whole],
        out_specs=whole,
        compiler_params=params,
        name="toeplitz",
    )(taps)


def conv_kernel(sig_ref, toep_ref, bias_ref, out_ref, x_ref, acc_ref):
    rows = sig_ref.shape[1]
    chans = rows // 2
    blocks = sig_ref.shape[0] // 2
    pad = lag_group - 1
    own = lax.axis_index("seq") * chans
    flat = bias_ref[...]
    at = lanes * lax.broadcasted_iota(jnp.int32, (chans,) + flat.shape, 1)
    at = at + lax.broadcasted_iota(jnp.int32, (chans,) + flat.shape, 2)
    want = own + lax.broadcasted_iota(jnp.int32, (chans,) + flat.shape, 0)
    bias = jnp.sum(jnp.where(at == want, flat[None], 0.0), axis=1)
    bias = jnp.sum(bias, axis=1, keepdims=True)
    bias = jnp.concatenate([bias, bias], axis=0)[None]
    row = lax.broadcasted_iota(jnp.int32, (block, block), 0)
    col = lax.broadcasted_iota(jnp.int32, (block, block), 1)
    flip = (row + col == block - 1).astype(f32).astype(bf16)
    x_ref[:pad] = jnp.zeros((pad,) + x_ref.shape[1:], bf16)
    pairs = sig_ref[...].reshape(blocks, 2, rows, lanes)
    x_ref[pad:, :chans, :lanes] = pairs[:, 0, :chans]
    x_ref[pad:, :chans, lanes:] = pairs[:, 1, :chans]
    wide = jnp.concatenate([pairs[:, 0, chans:], pairs[:, 1, chans:]], axis=2)
    wide = wide.reshape(blocks * chans, block)
    back = jnp.dot(wide, flip, preferred_element_type=f32).astype(bf16)
    for blk in range(blocks):
        src = (blocks - 1 - blk) * chans
        x_ref[pad + blk, chans:, :] = back[src : src + chans]
    for start in range(0, blocks, lag_group):
        count = blocks - start
        left = []
        right = []
        for lag in range(lag_group):
            seen = x_ref[pad - lag : pad - lag + count]
            left.append(seen.reshape(count * rows, block))
            at = block * (start + lag)
            right.append(toep_ref[:, at + lanes : at + lanes + block])
            right.append(toep_ref[:, at : at + block])
        prod = jnp.dot(
            jnp.concatenate(left, axis=1),
            jnp.concatenate(right, axis=0),
            preferred_element_type=f32,
        )
        if start == 0:
            acc_ref[...] = prod
        else:
            acc_ref[start * rows :, :] += prod
    vals = acc_ref[...].reshape(blocks, rows, block) + bias * x_ref[pad:].astype(f32)
    vals = vals.astype(bf16)
    wide = vals[:, chans:].reshape(blocks * chans, block)
    back = jnp.dot(wide, flip, preferred_element_type=f32).astype(bf16)
    for blk in range(blocks):
        out_ref[2 * blk, :chans] = vals[blk, :chans, :lanes]
        out_ref[2 * blk + 1, :chans] = vals[blk, :chans, lanes:]
        src = (blocks - 1 - blk) * chans
        out_ref[2 * blk, chans:] = back[src : src + chans, :lanes]
        out_ref[2 * blk + 1, chans:] = back[src : src + chans, lanes:]


def conv(signals, toep, bias):
    parts, rows, _ = signals.shape
    blocks = parts // 2
    return pl.pallas_call(
        conv_kernel,
        out_shape=jax.ShapeDtypeStruct(signals.shape, bf16),
        in_specs=[whole] * 3,
        out_specs=whole,
        scratch_shapes=[
            pltpu.VMEM((blocks + lag_group - 1, rows, block), bf16),
            pltpu.VMEM((blocks * rows, block), f32),
        ],
        compiler_params=params,
        name="conv",
    )(signals, toep, bias)


def cross_kernel(sig_ref, out_ref, w_ref, g_ref):
    chans = sig_ref.shape[1] // 2
    blocks = sig_ref.shape[0] // 2
    length = blocks * block
    half = blocks // 2
    span = half * chans
    pairs = sig_ref[...].reshape(blocks, 2, 2 * chans, lanes)
    mixed = jnp.concatenate([pairs[:, 0, :chans], pairs[:, 1, :chans]], axis=2)
    mixed = mixed.reshape(blocks * chans, block).astype(f32).T.astype(bf16)
    early = mixed[:, :span]
    both = jnp.concatenate([early, mixed[:, span:]], axis=0)
    wide = jnp.concatenate([pairs[:, 0, chans:], pairs[:, 1, chans:]], axis=2)
    w_ref[: blocks * chans] = wide.reshape(blocks * chans, block)
    w_ref[blocks * chans :] = jnp.zeros((span, block), bf16)
    for lag in range(half):
        low = lag * chans
        high = low + span
        far = jnp.dot(both, w_ref[high : high + span], preferred_element_type=f32)
        near = jnp.dot(early, w_ref[low : low + span], preferred_element_type=f32)
        near = near + far[block:]
        if lag == 0:
            row = lax.broadcasted_iota(jnp.int32, (block, block), 0)
            col = lax.broadcasted_iota(jnp.int32, (block, block), 1)
            near = jnp.where(col >= row, near, 0.0)
        g_ref[:, block * lag : block * lag + block] = near
        at = block * (half + lag)
        g_ref[:, at : at + block] = far[:block]
    size = block
    while size > 1:
        size //= 2
        moved = pltpu.roll(g_ref[size : 2 * size, :], length - size, 1)
        g_ref[:size, :] = g_ref[:size, :] + moved
    lines = length // lanes
    for line in range(lines):
        out_ref[line : line + 1, :] = g_ref[0:1, line * lanes : (line + 1) * lanes]
    prod = sig_ref[:, :chans].astype(f32) * sig_ref[:, chans:].astype(f32)
    total = jnp.sum(jnp.sum(prod, axis=0).T, axis=0, keepdims=True)
    rest = jnp.zeros((1, lanes - chans), f32)
    out_ref[lines : lines + 1, :] = jnp.concatenate([total, rest], axis=1)
    out_ref[lines + 1 :, :] = jnp.zeros((out_ref.shape[0] - lines - 1, lanes), f32)


def cross(signals):
    parts, rows, _ = signals.shape
    blocks = parts // 2
    chans = rows // 2
    return pl.pallas_call(
        cross_kernel,
        out_shape=jax.ShapeDtypeStruct((parts + 8, lanes), f32),
        in_specs=[whole],
        out_specs=whole,
        scratch_shapes=[
            pltpu.VMEM((blocks * chans * 3 // 2, block), bf16),
            pltpu.VMEM((block, blocks * block), f32),
        ],
        compiler_params=params,
        name="cross",
    )(signals)


def grads_kernel(back_ref, first_ref, value_ref, grad_ref, one_ref, two_ref, val_ref):
    chans = first_ref.shape[1]
    conv_vals = back_ref[:, :chans]
    back_vals = back_ref[:, chans:]
    one_ref[...] = times(back_vals, value_ref[...])
    two_ref[...] = times(grad_ref[...], conv_vals)
    val_ref[...] = times(back_vals, first_ref[...])


def grads(back, first, value, grad):
    parts, chans, width = first.shape
    step = parts // 4
    spec = pl.BlockSpec((step, chans, width), lambda i: (i, 0, 0))
    return pl.pallas_call(
        grads_kernel,
        grid=(parts // step,),
        out_shape=[jax.ShapeDtypeStruct(first.shape, bf16)] * 3,
        in_specs=[pl.BlockSpec((step, 2 * chans, width), lambda i: (i, 0, 0))] + [spec] * 3,
        out_specs=[spec] * 3,
        name="grads",
    )(back, first, value, grad)


def total_kernel(parts_ref, filter_ref, bias_ref):
    total = jnp.sum(parts_ref[...], axis=0)
    for line in range(filter_ref.shape[1] // lanes):
        filter_ref[:, line * lanes : (line + 1) * lanes] = total[line : line + 1]
    line = filter_ref.shape[1] // lanes
    bias_ref[...] = total[line : line + 1]


def per_device(first_gate, second_gate, value_proj, grad_out, filter_taps, skip_bias):
    ways = lax.axis_size("seq")
    chans = first_gate.shape[1] // ways
    shape = (ways, chans, lanes)
    first, second, value, grad = (
        arg.reshape(shape) for arg in (first_gate, second_gate, value_proj, grad_out)
    )
    toep = toeplitz(filter_taps)
    sent = gate(first, second, value, grad)
    signals = lax.all_to_all(sent, "seq", 0, 0, tiled=True)
    results = conv(signals, toep, skip_bias.reshape(-1, lanes))
    back = lax.all_to_all(results, "seq", 0, 0, tiled=True)
    partial = cross(signals)
    shares = lax.all_gather(partial, "dp")
    grad_filter, grad_bias = pl.pallas_call(
        total_kernel,
        out_shape=[
            jax.ShapeDtypeStruct(filter_taps.shape, f32),
            jax.ShapeDtypeStruct((1, lanes), f32),
        ],
        in_specs=[whole],
        out_specs=[whole] * 2,
        name="total",
    )(shares)
    outs = grads(back, first, value, grad)
    outs = [out.reshape(first_gate.shape) for out in outs]
    return (*outs, grad_filter, grad_bias[0, :chans])


def solution(mesh):
    return jax.shard_map(
        per_device,
        mesh=mesh,
        in_specs=(
            P("dp", None, "seq"),
            P("dp", None, "seq"),
            P("dp", None, "seq"),
            P("dp", None, "seq"),
            P("seq", None),
            P(),
        ),
        out_specs=(
            P("dp", None, "seq"),
            P("dp", None, "seq"),
            P("dp", None, "seq"),
            P("seq", None),
            P("seq"),
        ),
        check_vma=False,
    )
```

```python
import jax
import jax.numpy as jnp
from jax import lax
from jax.experimental import pallas as pl
from jax.experimental.pallas import tpu as pltpu
from jax.sharding import PartitionSpec as P

f32 = jnp.float32
bf16 = jnp.bfloat16
lanes = 128
block = 256
lag_group = 4
whole = pl.BlockSpec(memory_space=pltpu.VMEM)
gate_steps = 8
final_steps = 4
params = pltpu.CompilerParams(vmem_limit_bytes=24 << 20)


def times(left, right):
    return (left.astype(f32) * right.astype(f32)).astype(bf16)


def gate_kernel(first_in, second_in, value_in, grad_in, out_ref, *scratch):
    first_ref, second_ref, value_ref, grad_ref, held, sems, out_sems = scratch
    parts, chans, _ = first_in.shape
    step = parts // gate_steps
    pairs = (
        (first_in, first_ref),
        (value_in, value_ref),
        (grad_in, grad_ref),
        (second_in, second_ref),
    )
    loads = []
    for at in range(gate_steps):
        rows = pl.ds(at * step, step)
        lot = []
        for arg, (src, dst) in enumerate(pairs):
            copy = pltpu.make_async_copy(src.at[rows], dst.at[rows], sems.at[at, arg])
            copy.start()
            lot.append(copy)
        loads.append(lot)
    stores = []
    for at in range(gate_steps):
        rows = pl.ds(at * step, step)
        for copy in loads[at]:
            copy.wait()
        held[rows, :chans] = times(first_ref[rows], value_ref[rows])
        held[rows, chans:] = times(grad_ref[rows], second_ref[rows])
        copy = pltpu.make_async_copy(held.at[rows], out_ref.at[rows], out_sems.at[at])
        copy.start()
        stores.append(copy)
    for copy in stores:
        copy.wait()


def gate(first, second, value, grad):
    parts, chans, width = first.shape
    spec = pl.BlockSpec(memory_space=pltpu.HBM)
    return pl.pallas_call(
        gate_kernel,
        out_shape=jax.ShapeDtypeStruct((parts, 2 * chans, width), bf16),
        in_specs=[spec] * 4,
        out_specs=spec,
        scratch_shapes=[pltpu.VMEM(first.shape, bf16)] * 4
        + [
            pltpu.VMEM((parts, 2 * chans, width), bf16),
            pltpu.SemaphoreType.DMA((gate_steps, 4)),
            pltpu.SemaphoreType.DMA((gate_steps,)),
        ],
        compiler_params=pltpu.CompilerParams(vmem_limit_bytes=60 << 20),
        name="gate",
    )(first, second, value, grad)


def toeplitz_kernel(taps_ref, out_ref):
    length = taps_ref.shape[1]
    zero = jnp.zeros((1, lanes), f32)
    padded = jnp.concatenate([zero, taps_ref[...]], axis=1)
    rows = jnp.broadcast_to(padded, (8, length + lanes))
    rows = pltpu.roll(rows, 0, 1, stride=1, stride_axis=0)
    for top in range(0, lanes, 16):
        upper = rows if top == 0 else pltpu.roll(rows, top, 1)
        lower = pltpu.roll(rows, top + 8, 1)
        both = jnp.concatenate([upper, lower], axis=0)
        out_ref[top : top + 16, :] = both.astype(bf16)
    out_ref[:, :lanes] = jnp.zeros((lanes, lanes), bf16)


def toeplitz(taps):
    return pl.pallas_call(
        toeplitz_kernel,
        out_shape=jax.ShapeDtypeStruct((lanes, taps.shape[1] + lanes), bf16),
        in_specs=[whole],
        out_specs=whole,
        compiler_params=params,
        name="toeplitz",
    )(taps)


def conv_kernel(sig_ref, toep_ref, bias_ref, out_ref, x_ref, acc_ref):
    rows = sig_ref.shape[1]
    chans = rows // 2
    blocks = sig_ref.shape[0] // 2
    pad = lag_group - 1
    own = lax.axis_index("seq") * chans
    flat = bias_ref[...]
    at = lanes * lax.broadcasted_iota(jnp.int32, (chans,) + flat.shape, 1)
    at = at + lax.broadcasted_iota(jnp.int32, (chans,) + flat.shape, 2)
    want = own + lax.broadcasted_iota(jnp.int32, (chans,) + flat.shape, 0)
    bias = jnp.sum(jnp.where(at == want, flat[None], 0.0), axis=1)
    bias = jnp.sum(bias, axis=1, keepdims=True)
    bias = jnp.concatenate([bias, bias], axis=0)[None]
    row = lax.broadcasted_iota(jnp.int32, (block, block), 0)
    col = lax.broadcasted_iota(jnp.int32, (block, block), 1)
    flip = (row + col == block - 1).astype(f32).astype(bf16)
    x_ref[:pad] = jnp.zeros((pad,) + x_ref.shape[1:], bf16)
    pairs = sig_ref[...].reshape(blocks, 2, rows, lanes)
    x_ref[pad:, :chans, :lanes] = pairs[:, 0, :chans]
    x_ref[pad:, :chans, lanes:] = pairs[:, 1, :chans]
    wide = jnp.concatenate([pairs[:, 0, chans:], pairs[:, 1, chans:]], axis=2)
    wide = wide.reshape(blocks * chans, block)
    back = jnp.dot(wide, flip, preferred_element_type=f32).astype(bf16)
    for blk in range(blocks):
        src = (blocks - 1 - blk) * chans
        x_ref[pad + blk, chans:, :] = back[src : src + chans]
    for start in range(0, blocks, lag_group):
        count = blocks - start
        left = []
        right = []
        for lag in range(lag_group):
            seen = x_ref[pad - lag : pad - lag + count]
            left.append(seen.reshape(count * rows, block))
            at = block * (start + lag)
            right.append(toep_ref[:, at + lanes : at + lanes + block])
            right.append(toep_ref[:, at : at + block])
        prod = jnp.dot(
            jnp.concatenate(left, axis=1),
            jnp.concatenate(right, axis=0),
            preferred_element_type=f32,
        )
        if start == 0:
            acc_ref[...] = prod
        else:
            acc_ref[start * rows :, :] += prod
    vals = acc_ref[...].reshape(blocks, rows, block) + bias * x_ref[pad:].astype(f32)
    vals = vals.astype(bf16)
    wide = vals[:, chans:].reshape(blocks * chans, block)
    back = jnp.dot(wide, flip, preferred_element_type=f32).astype(bf16)
    for blk in range(blocks):
        out_ref[2 * blk, :chans] = vals[blk, :chans, :lanes]
        out_ref[2 * blk + 1, :chans] = vals[blk, :chans, lanes:]
        src = (blocks - 1 - blk) * chans
        out_ref[2 * blk, chans:] = back[src : src + chans, :lanes]
        out_ref[2 * blk + 1, chans:] = back[src : src + chans, lanes:]


def conv(signals, toep, bias):
    parts, rows, _ = signals.shape
    blocks = parts // 2
    return pl.pallas_call(
        conv_kernel,
        out_shape=jax.ShapeDtypeStruct(signals.shape, bf16),
        in_specs=[whole] * 3,
        out_specs=whole,
        scratch_shapes=[
            pltpu.VMEM((blocks + lag_group - 1, rows, block), bf16),
            pltpu.VMEM((blocks * rows, block), f32),
        ],
        compiler_params=params,
        name="conv",
    )(signals, toep, bias)


def cross_kernel(sig_ref, out_ref, w_ref, g_ref):
    chans = sig_ref.shape[1] // 2
    blocks = sig_ref.shape[0] // 2
    length = blocks * block
    half = blocks // 2
    span = half * chans
    pairs = sig_ref[...].reshape(blocks, 2, 2 * chans, lanes)
    mixed = jnp.concatenate([pairs[:, 0, :chans], pairs[:, 1, :chans]], axis=2)
    mixed = mixed.reshape(blocks * chans, block).astype(f32).T.astype(bf16)
    early = mixed[:, :span]
    both = jnp.concatenate([early, mixed[:, span:]], axis=0)
    wide = jnp.concatenate([pairs[:, 0, chans:], pairs[:, 1, chans:]], axis=2)
    w_ref[: blocks * chans] = wide.reshape(blocks * chans, block)
    w_ref[blocks * chans :] = jnp.zeros((span, block), bf16)
    for lag in range(half):
        low = lag * chans
        high = low + span
        far = jnp.dot(both, w_ref[high : high + span], preferred_element_type=f32)
        near = jnp.dot(early, w_ref[low : low + span], preferred_element_type=f32)
        near = near + far[block:]
        if lag == 0:
            row = lax.broadcasted_iota(jnp.int32, (block, block), 0)
            col = lax.broadcasted_iota(jnp.int32, (block, block), 1)
            near = jnp.where(col >= row, near, 0.0)
        g_ref[:, block * lag : block * lag + block] = near
        at = block * (half + lag)
        g_ref[:, at : at + block] = far[:block]
    size = block
    while size > 1:
        size //= 2
        moved = pltpu.roll(g_ref[size : 2 * size, :], length - size, 1)
        g_ref[:size, :] = g_ref[:size, :] + moved
    lines = length // lanes
    for line in range(lines):
        out_ref[line : line + 1, :] = g_ref[0:1, line * lanes : (line + 1) * lanes]
    prod = sig_ref[:, :chans].astype(f32) * sig_ref[:, chans:].astype(f32)
    total = jnp.sum(jnp.sum(prod, axis=0).T, axis=0, keepdims=True)
    rest = jnp.zeros((1, lanes - chans), f32)
    out_ref[lines : lines + 1, :] = jnp.concatenate([total, rest], axis=1)
    out_ref[lines + 1 :, :] = jnp.zeros((out_ref.shape[0] - lines - 1, lanes), f32)


def cross(signals):
    parts, rows, _ = signals.shape
    blocks = parts // 2
    chans = rows // 2
    return pl.pallas_call(
        cross_kernel,
        out_shape=jax.ShapeDtypeStruct((parts + 8, lanes), f32),
        in_specs=[whole],
        out_specs=whole,
        scratch_shapes=[
            pltpu.VMEM((blocks * chans * 3 // 2, block), bf16),
            pltpu.VMEM((block, blocks * block), f32),
        ],
        compiler_params=params,
        name="cross",
    )(signals)


def halve_kernel(pair_ref, half_ref, bias_ref):
    lines = half_ref.shape[0]
    core = lax.rem(lax.axis_index("dp"), 2)
    rows = pl.ds(pl.multiple_of(core * lines, lines), lines)
    half_ref[...] = (pair_ref[0, rows] + pair_ref[1, rows]).astype(bf16)
    line = pl.ds(2 * lines, 1)
    bias_ref[...] = (pair_ref[0, line] + pair_ref[1, line]).astype(bf16)


def halve(pair, lines):
    return pl.pallas_call(
        halve_kernel,
        out_shape=[
            jax.ShapeDtypeStruct((lines, lanes), bf16),
            jax.ShapeDtypeStruct((1, lanes), bf16),
        ],
        in_specs=[whole],
        out_specs=[whole] * 2,
        compiler_params=pltpu.CompilerParams(vmem_limit_bytes=4 << 20),
        name="halve",
    )(pair)


def final_kernel(back_ref, first_ref, value_ref, grad_ref, sums_ref, bias_ref, *rest):
    outs, filter_ref, total_ref, held, sems = rest[:3], rest[3], rest[4], rest[5:8], rest[8]
    parts, chans, _ = first_ref.shape
    step = parts // final_steps
    copies = []
    for at in range(final_steps):
        rows = pl.ds(at * step, step)
        back_vals = back_ref[rows, chans:]
        held[0][rows] = times(back_vals, value_ref[rows])
        held[1][rows] = times(grad_ref[rows], back_ref[rows, :chans])
        held[2][rows] = times(back_vals, first_ref[rows])
        for which in range(3):
            copy = pltpu.make_async_copy(
                held[which].at[rows], outs[which].at[rows], sems.at[at, which]
            )
            copy.start()
            copies.append(copy)
    sums = sums_ref[...].astype(f32)
    for line in range(sums.shape[0]):
        filter_ref[:, line * lanes : (line + 1) * lanes] = sums[line : line + 1]
    total_ref[...] = bias_ref[0, : total_ref.shape[0]].astype(f32)
    for copy in copies:
        copy.wait()


def final(back, first, value, grad, sums, bias):
    chans = first.shape[1]
    return pl.pallas_call(
        final_kernel,
        out_shape=[jax.ShapeDtypeStruct(first.shape, bf16)] * 3
        + [
            jax.ShapeDtypeStruct((1, sums.shape[0] * lanes), f32),
            jax.ShapeDtypeStruct((chans,), f32),
        ],
        in_specs=[whole] * 6,
        out_specs=[pl.BlockSpec(memory_space=pltpu.HBM)] * 3 + [whole] * 2,
        scratch_shapes=[pltpu.VMEM(first.shape, bf16)] * 3
        + [pltpu.SemaphoreType.DMA((final_steps, 3))],
        compiler_params=pltpu.CompilerParams(vmem_limit_bytes=8 << 20),
        name="final",
    )(back, first, value, grad, sums, bias)


def per_device(first_gate, second_gate, value_proj, grad_out, filter_taps, skip_bias):
    ways = lax.axis_size("seq")
    chans = first_gate.shape[1] // ways
    shape = (ways, chans, lanes)
    first, second, value, grad = (
        arg.reshape(shape) for arg in (first_gate, second_gate, value_proj, grad_out)
    )
    toep = toeplitz(filter_taps)
    sent = gate(first, second, value, grad)
    signals = lax.all_to_all(sent, "seq", 0, 0, tiled=True)
    results = conv(signals, toep, skip_bias.reshape(-1, lanes))
    back = lax.all_to_all(results, "seq", 0, 0, tiled=True)
    partial = cross(signals)
    ranks = lax.axis_size("dp")
    cores = [[at, at + 1] for at in range(0, ranks, 2)]
    chips = [list(range(core, ranks, 2)) for core in range(2)]
    pair = lax.all_gather(partial, "dp", axis_index_groups=cores)
    half, bias = halve(pair, filter_taps.shape[1] // lanes // 2)
    half, bias = lax.psum((half, bias), "dp", axis_index_groups=chips)
    sums = lax.all_gather(half, "dp", axis_index_groups=cores, tiled=True)
    outs = final(back, first, value, grad, sums, bias)
    return (*(out.reshape(first_gate.shape) for out in outs[:3]), *outs[3:])


def solution(mesh):
    return jax.shard_map(
        per_device,
        mesh=mesh,
        in_specs=(
            P("dp", None, "seq"),
            P("dp", None, "seq"),
            P("dp", None, "seq"),
            P("dp", None, "seq"),
            P("seq", None),
            P(),
        ),
        out_specs=(
            P("dp", None, "seq"),
            P("dp", None, "seq"),
            P("dp", None, "seq"),
            P("seq", None),
            P("seq"),
        ),
        check_vma=False,
    )
```

```python
import jax
import jax.numpy as jnp
from jax import lax
from jax.experimental import pallas as pl
from jax.experimental.pallas import tpu as pltpu
from jax.sharding import PartitionSpec as P

f32 = jnp.float32
bf16 = jnp.bfloat16
lanes = 128
block = 256
lag_group = 4
mixed_order = (
    13, 41, 12, 54, 44, 51, 37, 31, 57, 49, 53, 8, 40, 9, 5, 3,
    23, 62, 43, 7, 46, 18, 59, 10, 19, 48, 38, 60, 11, 17, 47, 52,
    28, 22, 55, 33, 15, 14, 61, 58, 20, 63, 34, 30, 56, 0, 6, 1,
    42, 26, 50, 2, 39, 25, 24, 32, 16, 21, 36, 29, 35, 27, 4, 45,
)
whole = pl.BlockSpec(memory_space=pltpu.VMEM)
gate_steps = 1
final_steps = 1
params = pltpu.CompilerParams(vmem_limit_bytes=24 << 20)


def seq_order(ways):
    return mixed_order if ways == len(mixed_order) else tuple(range(ways))


def slots(ways):
    order = seq_order(ways)
    return [order.index(which) for which in range(ways)]


def times(left, right):
    return (left.astype(f32) * right.astype(f32)).astype(bf16)


def gate_kernel(first_in, second_in, value_in, grad_in, out_ref, *scratch):
    first_ref, second_ref, value_ref, grad_ref, held, sems, out_sems = scratch
    parts, chans, _ = first_in.shape
    step = parts // gate_steps
    pairs = (
        (first_in, first_ref),
        (value_in, value_ref),
        (grad_in, grad_ref),
        (second_in, second_ref),
    )
    loads = []
    for at in range(gate_steps):
        rows = pl.ds(at * step, step)
        lot = []
        for arg, (src, dst) in enumerate(pairs):
            copy = pltpu.make_async_copy(src.at[rows], dst.at[rows], sems.at[at, arg])
            copy.start()
            lot.append(copy)
        loads.append(lot)
    for lot in loads:
        for copy in lot:
            copy.wait()
    stores = []
    order = seq_order(parts)
    for at in range(gate_steps):
        for slot in range(at * step, (at + 1) * step):
            which = order[slot]
            held[slot, :chans] = times(first_ref[which], value_ref[which])
            held[slot, chans:] = times(grad_ref[which], second_ref[which])
        rows = pl.ds(at * step, step)
        copy = pltpu.make_async_copy(held.at[rows], out_ref.at[rows], out_sems.at[at])
        copy.start()
        stores.append(copy)
    for copy in stores:
        copy.wait()


def gate(first, second, value, grad):
    parts, chans, width = first.shape
    spec = pl.BlockSpec(memory_space=pltpu.HBM)
    return pl.pallas_call(
        gate_kernel,
        out_shape=jax.ShapeDtypeStruct((parts, 2 * chans, width), bf16),
        in_specs=[spec] * 4,
        out_specs=spec,
        scratch_shapes=[pltpu.VMEM(first.shape, bf16)] * 4
        + [
            pltpu.VMEM((parts, 2 * chans, width), bf16),
            pltpu.SemaphoreType.DMA((gate_steps, 4)),
            pltpu.SemaphoreType.DMA((gate_steps,)),
        ],
        compiler_params=pltpu.CompilerParams(vmem_limit_bytes=60 << 20),
        name="gate",
    )(first, second, value, grad)


def toeplitz_kernel(taps_ref, out_ref):
    length = taps_ref.shape[1]
    zero = jnp.zeros((1, lanes), f32)
    padded = jnp.concatenate([zero, taps_ref[...]], axis=1)
    rows = jnp.broadcast_to(padded, (8, length + lanes))
    rows = pltpu.roll(rows, 0, 1, stride=1, stride_axis=0)
    for top in range(0, lanes, 16):
        upper = rows if top == 0 else pltpu.roll(rows, top, 1)
        lower = pltpu.roll(rows, top + 8, 1)
        both = jnp.concatenate([upper, lower], axis=0)
        out_ref[top : top + 16, :] = both.astype(bf16)
    out_ref[:, :lanes] = jnp.zeros((lanes, lanes), bf16)


def toeplitz(taps):
    return pl.pallas_call(
        toeplitz_kernel,
        out_shape=jax.ShapeDtypeStruct((lanes, taps.shape[1] + lanes), bf16),
        in_specs=[whole],
        out_specs=whole,
        compiler_params=params,
        name="toeplitz",
    )(taps)


def conv_kernel(sig_ref, toep_ref, bias_ref, out_ref, x_ref, acc_ref):
    rows = sig_ref.shape[1]
    chans = rows // 2
    blocks = sig_ref.shape[0] // 2
    pad = lag_group - 1
    own = lax.axis_index("seq") * chans
    flat = bias_ref[...]
    at = lanes * lax.broadcasted_iota(jnp.int32, (chans,) + flat.shape, 1)
    at = at + lax.broadcasted_iota(jnp.int32, (chans,) + flat.shape, 2)
    want = own + lax.broadcasted_iota(jnp.int32, (chans,) + flat.shape, 0)
    bias = jnp.sum(jnp.where(at == want, flat[None], 0.0), axis=1)
    bias = jnp.sum(bias, axis=1, keepdims=True)
    bias = bias[None, None]
    row = lax.broadcasted_iota(jnp.int32, (block, block), 0)
    col = lax.broadcasted_iota(jnp.int32, (block, block), 1)
    flip = (row + col == block - 1).astype(f32).astype(bf16)
    x_ref[:, :pad] = jnp.zeros((2, pad) + x_ref.shape[2:], bf16)
    slot = slots(2 * blocks)
    wide = []
    for blk in range(blocks):
        early, late = slot[2 * blk], slot[2 * blk + 1]
        x_ref[0, pad + blk, :, :lanes] = sig_ref[early, :chans]
        x_ref[0, pad + blk, :, lanes:] = sig_ref[late, :chans]
        wide.append(jnp.concatenate([sig_ref[early, chans:], sig_ref[late, chans:]], axis=1))
    wide = jnp.concatenate(wide[::-1], axis=0)
    back = jnp.dot(wide, flip, preferred_element_type=f32).astype(bf16)
    x_ref[1, pad:] = back.reshape(blocks, chans, block)
    for start in range(0, blocks, lag_group):
        count = blocks - start
        right = []
        for lag in range(lag_group):
            at = block * (start + lag)
            right.append(toep_ref[:, at + lanes : at + lanes + block])
            right.append(toep_ref[:, at : at + block])
        right = jnp.concatenate(right, axis=0)
        left = []
        for which in range(2):
            seen = [
                x_ref[which, pad - lag : pad - lag + count].reshape(count * chans, block)
                for lag in range(lag_group)
            ]
            left.append(jnp.concatenate(seen, axis=1))
        prod = jnp.dot(jnp.concatenate(left, axis=0), right, preferred_element_type=f32)
        prod = prod.reshape(2, count * chans, block)
        if start == 0:
            acc_ref[...] = prod
        else:
            acc_ref[:, start * chans :, :] += prod
    sums = acc_ref[...].reshape(2, blocks, chans, block)
    vals = (sums + bias * x_ref[:, pad:].astype(f32)).astype(bf16)
    wide = vals[1].reshape(blocks * chans, block)
    back = jnp.dot(wide, flip, preferred_element_type=f32).astype(bf16)
    for blk in range(blocks):
        early, late = slot[2 * blk], slot[2 * blk + 1]
        out_ref[early, :chans] = vals[0, blk, :, :lanes]
        out_ref[late, :chans] = vals[0, blk, :, lanes:]
        src = (blocks - 1 - blk) * chans
        out_ref[early, chans:] = back[src : src + chans, :lanes]
        out_ref[late, chans:] = back[src : src + chans, lanes:]


def conv(signals, toep, bias):
    parts, rows, _ = signals.shape
    blocks = parts // 2
    return pl.pallas_call(
        conv_kernel,
        out_shape=jax.ShapeDtypeStruct(signals.shape, bf16),
        in_specs=[whole] * 3,
        out_specs=whole,
        scratch_shapes=[
            pltpu.VMEM((2, blocks + lag_group - 1, rows // 2, block), bf16),
            pltpu.VMEM((2, blocks * rows // 2, block), f32),
        ],
        compiler_params=params,
        name="conv",
    )(signals, toep, bias)


def cross_kernel(sig_ref, out_ref, w_ref, g_ref):
    parts, rows, _ = sig_ref.shape
    chans = rows // 2
    length = parts * lanes
    slot = slots(parts)
    mixed = jnp.concatenate([sig_ref[slot[one], :chans] for one in range(parts)], axis=0)
    mixed = mixed.astype(f32).T.astype(bf16)
    for one in range(parts):
        part = sig_ref[slot[one], chans:]
        w_ref[one * chans : (one + 1) * chans, :lanes] = part
        if one:
            w_ref[(one - 1) * chans : one * chans, lanes:] = part
    w_ref[(parts - 1) * chans : parts * chans, lanes:] = jnp.zeros((chans, lanes), bf16)
    over = w_ref.shape[0] - parts * chans
    w_ref[parts * chans :] = jnp.zeros((over, block), bf16)
    for lag in range(0, parts, 2):
        depth = -(-(parts - lag) * chans // block) * block
        low = lag * chans
        near = jnp.dot(
            mixed[:, :depth], w_ref[low : low + depth], preferred_element_type=f32
        )
        if lag == 0:
            row = lax.broadcasted_iota(jnp.int32, near.shape, 0)
            col = lax.broadcasted_iota(jnp.int32, near.shape, 1)
            near = jnp.where(col >= row, near, 0.0)
        g_ref[:, lanes * lag : lanes * lag + block] = near
    size = lanes
    while size > 1:
        size //= 2
        moved = pltpu.roll(g_ref[size : 2 * size, :], length - size, 1)
        g_ref[:size, :] = g_ref[:size, :] + moved
    for one in range(parts):
        out_ref[one : one + 1, :] = g_ref[0:1, one * lanes : (one + 1) * lanes]
    prod = sig_ref[:, :chans].astype(f32) * sig_ref[:, chans:].astype(f32)
    total = jnp.sum(jnp.sum(prod, axis=0).T, axis=0, keepdims=True)
    rest = jnp.zeros((1, lanes - chans), f32)
    out_ref[parts : parts + 1, :] = jnp.concatenate([total, rest], axis=1)
    out_ref[parts + 1 :, :] = jnp.zeros((out_ref.shape[0] - parts - 1, lanes), f32)


def cross(signals):
    parts, rows, _ = signals.shape
    chans = rows // 2
    return pl.pallas_call(
        cross_kernel,
        out_shape=jax.ShapeDtypeStruct((parts + 8, lanes), f32),
        in_specs=[whole],
        out_specs=whole,
        scratch_shapes=[
            pltpu.VMEM((parts * chans + block, block), bf16),
            pltpu.VMEM((lanes, parts * lanes), f32),
        ],
        compiler_params=params,
        name="cross",
    )(signals)


def halve_kernel(pair_ref, half_ref, bias_ref):
    lines = half_ref.shape[0]
    core = lax.rem(lax.axis_index("dp"), 2)
    rows = pl.ds(pl.multiple_of(core * lines, lines), lines)
    half_ref[...] = (pair_ref[0, rows] + pair_ref[1, rows]).astype(bf16)
    line = pl.ds(2 * lines, 1)
    bias_ref[...] = (pair_ref[0, line] + pair_ref[1, line]).astype(bf16)


def halve(pair, lines):
    return pl.pallas_call(
        halve_kernel,
        out_shape=[
            jax.ShapeDtypeStruct((lines, lanes), bf16),
            jax.ShapeDtypeStruct((1, lanes), bf16),
        ],
        in_specs=[whole],
        out_specs=[whole] * 2,
        compiler_params=pltpu.CompilerParams(vmem_limit_bytes=4 << 20),
        name="halve",
    )(pair)


def final_kernel(back_ref, first_ref, value_ref, grad_ref, sums_ref, bias_ref, *rest):
    outs, held, sems = rest[:5], rest[5:10], rest[10]
    parts, chans, _ = first_ref.shape
    step = parts // final_steps
    slot = slots(parts)
    copies = []
    for at in range(final_steps):
        for one in range(at * step, (at + 1) * step):
            back_vals = back_ref[slot[one], chans:]
            held[0][one] = times(back_vals, value_ref[one])
            held[1][one] = times(grad_ref[one], back_ref[slot[one], :chans])
            held[2][one] = times(back_vals, first_ref[one])
        rows = pl.ds(at * step, step)
        for which in range(3):
            copy = pltpu.make_async_copy(
                held[which].at[rows], outs[which].at[rows], sems.at[at, which]
            )
            copy.start()
            copies.append(copy)
    sums = sums_ref[...].astype(f32)
    for line in range(sums.shape[0]):
        held[3][:, line * lanes : (line + 1) * lanes] = sums[line : line + 1]
    held[4][...] = bias_ref[0, :chans].astype(f32)
    for which in (3, 4):
        copy = pltpu.make_async_copy(held[which], outs[which], sems.at[final_steps, which - 3])
        copy.start()
        copies.append(copy)
    for copy in copies:
        copy.wait()


def final(back, first, value, grad, sums, bias):
    chans = first.shape[1]
    line = (1, sums.shape[0] * lanes)
    shapes = [(first.shape, bf16)] * 3 + [(line, f32), ((chans,), f32)]
    return pl.pallas_call(
        final_kernel,
        out_shape=[jax.ShapeDtypeStruct(*shape) for shape in shapes],
        in_specs=[whole] * 6,
        out_specs=[pl.BlockSpec(memory_space=pltpu.HBM)] * 5,
        scratch_shapes=[pltpu.VMEM(*shape) for shape in shapes]
        + [pltpu.SemaphoreType.DMA((final_steps + 1, 3))],
        compiler_params=pltpu.CompilerParams(vmem_limit_bytes=8 << 20),
        name="final",
    )(back, first, value, grad, sums, bias)


def per_device(first_gate, second_gate, value_proj, grad_out, filter_taps, skip_bias):
    ways = lax.axis_size("seq")
    chans = first_gate.shape[1] // ways
    shape = (ways, chans, lanes)
    first, second, value, grad = (
        arg.reshape(shape) for arg in (first_gate, second_gate, value_proj, grad_out)
    )
    toep = toeplitz(filter_taps)
    sent = gate(first, second, value, grad)
    order = [seq_order(ways)]
    signals = lax.all_to_all(sent, "seq", 0, 0, axis_index_groups=order, tiled=True)
    results = conv(signals, toep, skip_bias.reshape(-1, lanes))
    back = lax.all_to_all(results, "seq", 0, 0, axis_index_groups=order, tiled=True)
    partial = cross(signals)
    ranks = lax.axis_size("dp")
    cores = [[at, at + 1] for at in range(0, ranks, 2)]
    chips = [list(range(core, ranks, 2)) for core in range(2)]
    pair = lax.all_gather(partial, "dp", axis_index_groups=cores)
    half, bias = halve(pair, filter_taps.shape[1] // lanes // 2)
    half, bias = lax.psum((half, bias), "dp", axis_index_groups=chips)
    sums = lax.all_gather(half, "dp", axis_index_groups=cores, tiled=True)
    outs = final(back, first, value, grad, sums, bias)
    return (*(out.reshape(first_gate.shape) for out in outs[:3]), *outs[3:])


def solution(mesh):
    return jax.shard_map(
        per_device,
        mesh=mesh,
        in_specs=(
            P("dp", None, "seq"),
            P("dp", None, "seq"),
            P("dp", None, "seq"),
            P("dp", None, "seq"),
            P("seq", None),
            P(),
        ),
        out_specs=(
            P("dp", None, "seq"),
            P("dp", None, "seq"),
            P("dp", None, "seq"),
            P("seq", None),
            P("seq"),
        ),
        check_vma=False,
    )
```

```python
import jax
import jax.numpy as jnp
from jax import lax
from jax.experimental import pallas as pl
from jax.experimental.pallas import tpu as pltpu
from jax.sharding import PartitionSpec as P

f32 = jnp.float32
bf16 = jnp.bfloat16
lanes = 128
block = 256
lag_group = 4
mixed_order = (
    17, 50, 1, 15, 12, 14, 30, 41, 37, 57, 60, 21, 35, 8, 61, 10,
    22, 7, 44, 63, 46, 20, 55, 0, 31, 13, 58, 49, 19, 16, 25, 54,
    36, 48, 52, 45, 34, 4, 26, 5, 3, 9, 51, 27, 24, 18, 38, 29,
    43, 6, 33, 28, 23, 56, 2, 32, 40, 62, 47, 53, 42, 39, 59, 11,
)
whole = pl.BlockSpec(memory_space=pltpu.VMEM)
gate_steps = 1
final_steps = 1
params = pltpu.CompilerParams(vmem_limit_bytes=24 << 20)


def seq_order(ways):
    return mixed_order if ways == len(mixed_order) else tuple(range(ways))


def slots(ways):
    order = seq_order(ways)
    return [order.index(which) for which in range(ways)]


def times(left, right):
    return (left.astype(f32) * right.astype(f32)).astype(bf16)


def gate_kernel(first_in, second_in, value_in, grad_in, out_ref, *scratch):
    first_ref, second_ref, value_ref, grad_ref, held, sems, out_sems = scratch
    parts, chans, _ = first_in.shape
    step = parts // gate_steps
    pairs = (
        (first_in, first_ref),
        (value_in, value_ref),
        (grad_in, grad_ref),
        (second_in, second_ref),
    )
    loads = []
    for at in range(gate_steps):
        rows = pl.ds(at * step, step)
        lot = []
        for arg, (src, dst) in enumerate(pairs):
            copy = pltpu.make_async_copy(src.at[rows], dst.at[rows], sems.at[at, arg])
            copy.start()
            lot.append(copy)
        loads.append(lot)
    for lot in loads:
        for copy in lot:
            copy.wait()
    stores = []
    order = seq_order(parts)
    for at in range(gate_steps):
        for slot in range(at * step, (at + 1) * step):
            which = order[slot]
            held[slot, :chans] = times(first_ref[which], value_ref[which])
            held[slot, chans:] = times(grad_ref[which], second_ref[which])
        rows = pl.ds(at * step, step)
        copy = pltpu.make_async_copy(held.at[rows], out_ref.at[rows], out_sems.at[at])
        copy.start()
        stores.append(copy)
    for copy in stores:
        copy.wait()


def gate(first, second, value, grad):
    parts, chans, width = first.shape
    spec = pl.BlockSpec(memory_space=pltpu.HBM)
    return pl.pallas_call(
        gate_kernel,
        out_shape=jax.ShapeDtypeStruct((parts, 2 * chans, width), bf16),
        in_specs=[spec] * 4,
        out_specs=spec,
        scratch_shapes=[pltpu.VMEM(first.shape, bf16)] * 4
        + [
            pltpu.VMEM((parts, 2 * chans, width), bf16),
            pltpu.SemaphoreType.DMA((gate_steps, 4)),
            pltpu.SemaphoreType.DMA((gate_steps,)),
        ],
        compiler_params=pltpu.CompilerParams(vmem_limit_bytes=60 << 20),
        name="gate",
    )(first, second, value, grad)


def toeplitz_kernel(taps_ref, out_ref):
    length = taps_ref.shape[1]
    zero = jnp.zeros((1, lanes), f32)
    padded = jnp.concatenate([zero, taps_ref[...]], axis=1)
    rows = jnp.broadcast_to(padded, (8, length + lanes))
    rows = pltpu.roll(rows, 0, 1, stride=1, stride_axis=0)
    for top in range(0, lanes, 16):
        upper = rows if top == 0 else pltpu.roll(rows, top, 1)
        lower = pltpu.roll(rows, top + 8, 1)
        both = jnp.concatenate([upper, lower], axis=0)
        out_ref[top : top + 16, :] = both.astype(bf16)
    out_ref[:, :lanes] = jnp.zeros((lanes, lanes), bf16)


def toeplitz(taps):
    return pl.pallas_call(
        toeplitz_kernel,
        out_shape=jax.ShapeDtypeStruct((lanes, taps.shape[1] + lanes), bf16),
        in_specs=[whole],
        out_specs=whole,
        compiler_params=params,
        name="toeplitz",
    )(taps)


def conv_kernel(sig_ref, toep_ref, bias_ref, out_ref, x_ref, acc_ref):
    rows = sig_ref.shape[1]
    chans = rows // 2
    blocks = sig_ref.shape[0] // 2
    pad = lag_group - 1
    own = lax.axis_index("seq") * chans
    flat = bias_ref[...]
    at = lanes * lax.broadcasted_iota(jnp.int32, (chans,) + flat.shape, 1)
    at = at + lax.broadcasted_iota(jnp.int32, (chans,) + flat.shape, 2)
    want = own + lax.broadcasted_iota(jnp.int32, (chans,) + flat.shape, 0)
    bias = jnp.sum(jnp.where(at == want, flat[None], 0.0), axis=1)
    bias = jnp.sum(bias, axis=1, keepdims=True)
    bias = bias[None, None]
    row = lax.broadcasted_iota(jnp.int32, (block, block), 0)
    col = lax.broadcasted_iota(jnp.int32, (block, block), 1)
    flip = (row + col == block - 1).astype(f32).astype(bf16)
    x_ref[:, :pad] = jnp.zeros((2, pad) + x_ref.shape[2:], bf16)
    slot = slots(2 * blocks)
    wide = []
    for blk in range(blocks):
        early, late = slot[2 * blk], slot[2 * blk + 1]
        x_ref[0, pad + blk, :, :lanes] = sig_ref[early, :chans]
        x_ref[0, pad + blk, :, lanes:] = sig_ref[late, :chans]
        wide.append(jnp.concatenate([sig_ref[early, chans:], sig_ref[late, chans:]], axis=1))
    wide = jnp.concatenate(wide[::-1], axis=0)
    back = jnp.dot(wide, flip, preferred_element_type=f32).astype(bf16)
    x_ref[1, pad:] = back.reshape(blocks, chans, block)
    for start in range(0, blocks, lag_group):
        count = blocks - start
        right = []
        for lag in range(lag_group):
            at = block * (start + lag)
            right.append(toep_ref[:, at + lanes : at + lanes + block])
            right.append(toep_ref[:, at : at + block])
        right = jnp.concatenate(right, axis=0)
        left = []
        for which in range(2):
            seen = [
                x_ref[which, pad - lag : pad - lag + count].reshape(count * chans, block)
                for lag in range(lag_group)
            ]
            left.append(jnp.concatenate(seen, axis=1))
        prod = jnp.dot(jnp.concatenate(left, axis=0), right, preferred_element_type=f32)
        prod = prod.reshape(2, count * chans, block)
        if start == 0:
            acc_ref[...] = prod
        else:
            acc_ref[:, start * chans :, :] += prod
    sums = acc_ref[...].reshape(2, blocks, chans, block)
    vals = (sums + bias * x_ref[:, pad:].astype(f32)).astype(bf16)
    wide = vals[1].reshape(blocks * chans, block)
    back = jnp.dot(wide, flip, preferred_element_type=f32).astype(bf16)
    for blk in range(blocks):
        early, late = slot[2 * blk], slot[2 * blk + 1]
        out_ref[early, :chans] = vals[0, blk, :, :lanes]
        out_ref[late, :chans] = vals[0, blk, :, lanes:]
        src = (blocks - 1 - blk) * chans
        out_ref[early, chans:] = back[src : src + chans, :lanes]
        out_ref[late, chans:] = back[src : src + chans, lanes:]


def conv(signals, toep, bias):
    parts, rows, _ = signals.shape
    blocks = parts // 2
    return pl.pallas_call(
        conv_kernel,
        out_shape=jax.ShapeDtypeStruct(signals.shape, bf16),
        in_specs=[whole] * 3,
        out_specs=whole,
        scratch_shapes=[
            pltpu.VMEM((2, blocks + lag_group - 1, rows // 2, block), bf16),
            pltpu.VMEM((2, blocks * rows // 2, block), f32),
        ],
        compiler_params=params,
        name="conv",
    )(signals, toep, bias)


def cross_kernel(sig_ref, out_ref, w_ref, g_ref):
    parts, rows, _ = sig_ref.shape
    chans = rows // 2
    length = parts * lanes
    slot = slots(parts)
    mixed = jnp.concatenate([sig_ref[slot[one], :chans] for one in range(parts)], axis=0)
    mixed = mixed.astype(f32).T.astype(bf16)
    for one in range(parts):
        part = sig_ref[slot[one], chans:]
        w_ref[one * chans : (one + 1) * chans, :lanes] = part
        if one:
            w_ref[(one - 1) * chans : one * chans, lanes:] = part
    w_ref[(parts - 1) * chans : parts * chans, lanes:] = jnp.zeros((chans, lanes), bf16)
    over = w_ref.shape[0] - parts * chans
    w_ref[parts * chans :] = jnp.zeros((over, block), bf16)
    for lag in range(0, parts, 2):
        depth = -(-(parts - lag) * chans // block) * block
        low = lag * chans
        near = jnp.dot(
            mixed[:, :depth], w_ref[low : low + depth], preferred_element_type=f32
        )
        if lag == 0:
            row = lax.broadcasted_iota(jnp.int32, near.shape, 0)
            col = lax.broadcasted_iota(jnp.int32, near.shape, 1)
            near = jnp.where(col >= row, near, 0.0)
        g_ref[:, lanes * lag : lanes * lag + block] = near
    total = g_ref[:8, :]
    for top in range(8, lanes, 8):
        total = total + pltpu.roll(g_ref[top : top + 8, :], length - top, 1)
    size = 8
    while size > 1:
        size //= 2
        total = total[:size] + pltpu.roll(total[size : 2 * size], length - size, 1)
    for one in range(parts):
        out_ref[one : one + 1, :] = total[:, one * lanes : (one + 1) * lanes]
    prod = sig_ref[:, :chans].astype(f32) * sig_ref[:, chans:].astype(f32)
    bias = jnp.sum(jnp.sum(prod, axis=0).T, axis=0, keepdims=True)
    rest = jnp.zeros((1, lanes - chans), f32)
    out_ref[parts : parts + 1, :] = jnp.concatenate([bias, rest], axis=1)
    out_ref[parts + 1 :, :] = jnp.zeros((out_ref.shape[0] - parts - 1, lanes), f32)


def cross(signals):
    parts, rows, _ = signals.shape
    chans = rows // 2
    return pl.pallas_call(
        cross_kernel,
        out_shape=jax.ShapeDtypeStruct((parts + 8, lanes), f32),
        in_specs=[whole],
        out_specs=whole,
        scratch_shapes=[
            pltpu.VMEM((parts * chans + block, block), bf16),
            pltpu.VMEM((lanes, parts * lanes), f32),
        ],
        compiler_params=params,
        name="cross",
    )(signals)


def halve_kernel(pair_ref, half_ref, bias_ref):
    lines = half_ref.shape[0]
    core = lax.rem(lax.axis_index("dp"), 2)
    rows = pl.ds(pl.multiple_of(core * lines, lines), lines)
    half_ref[...] = (pair_ref[0, rows] + pair_ref[1, rows]).astype(bf16)
    line = pl.ds(2 * lines, 1)
    bias_ref[...] = (pair_ref[0, line] + pair_ref[1, line]).astype(bf16)


def halve(pair, lines):
    return pl.pallas_call(
        halve_kernel,
        out_shape=[
            jax.ShapeDtypeStruct((lines, lanes), bf16),
            jax.ShapeDtypeStruct((1, lanes), bf16),
        ],
        in_specs=[whole],
        out_specs=[whole] * 2,
        compiler_params=pltpu.CompilerParams(vmem_limit_bytes=4 << 20),
        name="halve",
    )(pair)


def final_kernel(back_ref, first_ref, value_ref, grad_ref, sums_ref, bias_ref, *rest):
    outs, held, sems = rest[:5], rest[5:10], rest[10]
    parts, chans, _ = first_ref.shape
    step = parts // final_steps
    slot = slots(parts)
    copies = []
    for at in range(final_steps):
        for one in range(at * step, (at + 1) * step):
            back_vals = back_ref[slot[one], chans:]
            held[0][one] = times(back_vals, value_ref[one])
            held[1][one] = times(grad_ref[one], back_ref[slot[one], :chans])
            held[2][one] = times(back_vals, first_ref[one])
        rows = pl.ds(at * step, step)
        for which in range(3):
            copy = pltpu.make_async_copy(
                held[which].at[rows], outs[which].at[rows], sems.at[at, which]
            )
            copy.start()
            copies.append(copy)
    sums = sums_ref[...].astype(f32)
    for line in range(sums.shape[0]):
        held[3][:, line * lanes : (line + 1) * lanes] = sums[line : line + 1]
    held[4][...] = bias_ref[0, :chans].astype(f32)
    for which in (3, 4):
        copy = pltpu.make_async_copy(held[which], outs[which], sems.at[final_steps, which - 3])
        copy.start()
        copies.append(copy)
    for copy in copies:
        copy.wait()


def final(back, first, value, grad, sums, bias):
    chans = first.shape[1]
    line = (1, sums.shape[0] * lanes)
    shapes = [(first.shape, bf16)] * 3 + [(line, f32), ((chans,), f32)]
    return pl.pallas_call(
        final_kernel,
        out_shape=[jax.ShapeDtypeStruct(*shape) for shape in shapes],
        in_specs=[whole] * 6,
        out_specs=[pl.BlockSpec(memory_space=pltpu.HBM)] * 5,
        scratch_shapes=[pltpu.VMEM(*shape) for shape in shapes]
        + [pltpu.SemaphoreType.DMA((final_steps + 1, 3))],
        compiler_params=pltpu.CompilerParams(vmem_limit_bytes=8 << 20),
        name="final",
    )(back, first, value, grad, sums, bias)


def per_device(first_gate, second_gate, value_proj, grad_out, filter_taps, skip_bias):
    ways = lax.axis_size("seq")
    chans = first_gate.shape[1] // ways
    shape = (ways, chans, lanes)
    first, second, value, grad = (
        arg.reshape(shape) for arg in (first_gate, second_gate, value_proj, grad_out)
    )
    toep = toeplitz(filter_taps)
    sent = gate(first, second, value, grad)
    order = [seq_order(ways)]
    signals = lax.all_to_all(sent, "seq", 0, 0, axis_index_groups=order, tiled=True)
    results = conv(signals, toep, skip_bias.reshape(-1, lanes))
    back = lax.all_to_all(results, "seq", 0, 0, axis_index_groups=order, tiled=True)
    partial = cross(signals)
    ranks = lax.axis_size("dp")
    cores = [[at, at + 1] for at in range(0, ranks, 2)]
    chips = [list(range(core, ranks, 2)) for core in range(2)]
    pair = lax.all_gather(partial, "dp", axis_index_groups=cores)
    half, bias = halve(pair, filter_taps.shape[1] // lanes // 2)
    half, bias = lax.psum((half, bias), "dp", axis_index_groups=chips)
    sums = lax.all_gather(half, "dp", axis_index_groups=cores, tiled=True)
    outs = final(back, first, value, grad, sums, bias)
    return (*(out.reshape(first_gate.shape) for out in outs[:3]), *outs[3:])


def solution(mesh):
    return jax.shard_map(
        per_device,
        mesh=mesh,
        in_specs=(
            P("dp", None, "seq"),
            P("dp", None, "seq"),
            P("dp", None, "seq"),
            P("dp", None, "seq"),
            P("seq", None),
            P(),
        ),
        out_specs=(
            P("dp", None, "seq"),
            P("dp", None, "seq"),
            P("dp", None, "seq"),
            P("seq", None),
            P("seq"),
        ),
        check_vma=False,
    )
```

```python
import jax
import jax.numpy as jnp
from jax import lax
from jax.experimental import pallas as pl
from jax.experimental.pallas import tpu as pltpu
from jax.sharding import PartitionSpec as P

f32 = jnp.float32
bf16 = jnp.bfloat16
lanes = 128
block = 256
lag_group = 4
mixed_order = (
    17, 50, 1, 15, 12, 14, 30, 41, 37, 57, 60, 21, 35, 8, 61, 4,
    22, 7, 44, 63, 46, 20, 55, 0, 31, 13, 58, 43, 19, 16, 25, 54,
    36, 48, 52, 45, 34, 10, 26, 5, 3, 9, 2, 27, 28, 47, 38, 29,
    49, 6, 33, 24, 23, 56, 51, 32, 40, 62, 18, 53, 42, 39, 59, 11,
)
whole = pl.BlockSpec(memory_space=pltpu.VMEM)
gate_steps = 1
final_steps = 1
params = pltpu.CompilerParams(vmem_limit_bytes=24 << 20)


def seq_order(ways):
    return mixed_order if ways == len(mixed_order) else tuple(range(ways))


def slots(ways):
    order = seq_order(ways)
    return [order.index(which) for which in range(ways)]


def times(left, right):
    return (left.astype(f32) * right.astype(f32)).astype(bf16)


def gate_kernel(first_in, second_in, value_in, grad_in, out_ref, *scratch):
    first_ref, second_ref, value_ref, grad_ref, held, sems, out_sems = scratch
    parts, chans, _ = first_in.shape
    step = parts // gate_steps
    pairs = (
        (first_in, first_ref),
        (value_in, value_ref),
        (grad_in, grad_ref),
        (second_in, second_ref),
    )
    loads = []
    for at in range(gate_steps):
        rows = pl.ds(at * step, step)
        lot = []
        for arg, (src, dst) in enumerate(pairs):
            copy = pltpu.make_async_copy(src.at[rows], dst.at[rows], sems.at[at, arg])
            copy.start()
            lot.append(copy)
        loads.append(lot)
    for lot in loads:
        for copy in lot:
            copy.wait()
    stores = []
    order = seq_order(parts)
    for at in range(gate_steps):
        for slot in range(at * step, (at + 1) * step):
            which = order[slot]
            held[slot, :chans] = times(first_ref[which], value_ref[which])
            held[slot, chans:] = times(grad_ref[which], second_ref[which])
        rows = pl.ds(at * step, step)
        copy = pltpu.make_async_copy(held.at[rows], out_ref.at[rows], out_sems.at[at])
        copy.start()
        stores.append(copy)
    for copy in stores:
        copy.wait()


def gate(first, second, value, grad):
    parts, chans, width = first.shape
    spec = pl.BlockSpec(memory_space=pltpu.HBM)
    return pl.pallas_call(
        gate_kernel,
        out_shape=jax.ShapeDtypeStruct((parts, 2 * chans, width), bf16),
        in_specs=[spec] * 4,
        out_specs=spec,
        scratch_shapes=[pltpu.VMEM(first.shape, bf16)] * 4
        + [
            pltpu.VMEM((parts, 2 * chans, width), bf16),
            pltpu.SemaphoreType.DMA((gate_steps, 4)),
            pltpu.SemaphoreType.DMA((gate_steps,)),
        ],
        compiler_params=pltpu.CompilerParams(vmem_limit_bytes=60 << 20),
        name="gate",
    )(first, second, value, grad)


def toeplitz_kernel(taps_ref, out_ref):
    length = taps_ref.shape[1]
    zero = jnp.zeros((1, lanes), f32)
    padded = jnp.concatenate([zero, taps_ref[...]], axis=1)
    rows = jnp.broadcast_to(padded, (8, length + lanes))
    rows = pltpu.roll(rows, 0, 1, stride=1, stride_axis=0)
    for top in range(0, lanes, 16):
        upper = rows if top == 0 else pltpu.roll(rows, top, 1)
        lower = pltpu.roll(rows, top + 8, 1)
        both = jnp.concatenate([upper, lower], axis=0)
        out_ref[top : top + 16, :] = both.astype(bf16)
    out_ref[:, :lanes] = jnp.zeros((lanes, lanes), bf16)


def toeplitz(taps):
    return pl.pallas_call(
        toeplitz_kernel,
        out_shape=jax.ShapeDtypeStruct((lanes, taps.shape[1] + lanes), bf16),
        in_specs=[whole],
        out_specs=whole,
        compiler_params=params,
        name="toeplitz",
    )(taps)


def conv_kernel(sig_ref, toep_ref, bias_ref, out_ref, x_ref, acc_ref):
    rows = sig_ref.shape[1]
    chans = rows // 2
    blocks = sig_ref.shape[0] // 2
    pad = lag_group - 1
    own = lax.axis_index("seq") * chans
    flat = bias_ref[...]
    at = lanes * lax.broadcasted_iota(jnp.int32, (chans,) + flat.shape, 1)
    at = at + lax.broadcasted_iota(jnp.int32, (chans,) + flat.shape, 2)
    want = own + lax.broadcasted_iota(jnp.int32, (chans,) + flat.shape, 0)
    bias = jnp.sum(jnp.where(at == want, flat[None], 0.0), axis=1)
    bias = jnp.sum(bias, axis=1, keepdims=True)
    bias = bias[None, None]
    row = lax.broadcasted_iota(jnp.int32, (block, block), 0)
    col = lax.broadcasted_iota(jnp.int32, (block, block), 1)
    flip = (row + col == block - 1).astype(f32).astype(bf16)
    x_ref[:, :pad] = jnp.zeros((2, pad) + x_ref.shape[2:], bf16)
    slot = slots(2 * blocks)
    wide = []
    for blk in range(blocks):
        early, late = slot[2 * blk], slot[2 * blk + 1]
        x_ref[0, pad + blk, :, :lanes] = sig_ref[early, :chans]
        x_ref[0, pad + blk, :, lanes:] = sig_ref[late, :chans]
        wide.append(jnp.concatenate([sig_ref[early, chans:], sig_ref[late, chans:]], axis=1))
    wide = jnp.concatenate(wide[::-1], axis=0)
    back = jnp.dot(wide, flip, preferred_element_type=f32).astype(bf16)
    x_ref[1, pad:] = back.reshape(blocks, chans, block)
    for start in range(0, blocks, lag_group):
        count = blocks - start
        right = []
        for lag in range(lag_group):
            at = block * (start + lag)
            right.append(toep_ref[:, at + lanes : at + lanes + block])
            right.append(toep_ref[:, at : at + block])
        right = jnp.concatenate(right, axis=0)
        left = []
        for which in range(2):
            seen = [
                x_ref[which, pad - lag : pad - lag + count].reshape(count * chans, block)
                for lag in range(lag_group)
            ]
            left.append(jnp.concatenate(seen, axis=1))
        prod = jnp.dot(jnp.concatenate(left, axis=0), right, preferred_element_type=f32)
        prod = prod.reshape(2, count * chans, block)
        if start == 0:
            acc_ref[...] = prod
        else:
            acc_ref[:, start * chans :, :] += prod
    sums = acc_ref[...].reshape(2, blocks, chans, block)
    vals = (sums + bias * x_ref[:, pad:].astype(f32)).astype(bf16)
    wide = vals[1].reshape(blocks * chans, block)
    back = jnp.dot(wide, flip, preferred_element_type=f32).astype(bf16)
    for blk in range(blocks):
        early, late = slot[2 * blk], slot[2 * blk + 1]
        out_ref[early, :chans] = vals[0, blk, :, :lanes]
        out_ref[late, :chans] = vals[0, blk, :, lanes:]
        src = (blocks - 1 - blk) * chans
        out_ref[early, chans:] = back[src : src + chans, :lanes]
        out_ref[late, chans:] = back[src : src + chans, lanes:]


def conv(signals, toep, bias):
    parts, rows, _ = signals.shape
    blocks = parts // 2
    return pl.pallas_call(
        conv_kernel,
        out_shape=jax.ShapeDtypeStruct(signals.shape, bf16),
        in_specs=[whole] * 3,
        out_specs=whole,
        scratch_shapes=[
            pltpu.VMEM((2, blocks + lag_group - 1, rows // 2, block), bf16),
            pltpu.VMEM((2, blocks * rows // 2, block), f32),
        ],
        compiler_params=params,
        name="conv",
    )(signals, toep, bias)


def cross_kernel(sig_ref, out_ref, w_ref, g_ref):
    parts, rows, _ = sig_ref.shape
    chans = rows // 2
    length = parts * lanes
    slot = slots(parts)
    mixed = jnp.concatenate([sig_ref[slot[one], :chans] for one in range(parts)], axis=0)
    mixed = mixed.astype(f32).T.astype(bf16)
    for one in range(parts):
        part = sig_ref[slot[one], chans:]
        w_ref[one * chans : (one + 1) * chans, :lanes] = part
        if one:
            w_ref[(one - 1) * chans : one * chans, lanes:] = part
    w_ref[(parts - 1) * chans : parts * chans, lanes:] = jnp.zeros((chans, lanes), bf16)
    over = w_ref.shape[0] - parts * chans
    w_ref[parts * chans :] = jnp.zeros((over, block), bf16)
    for lag in range(0, parts, 2):
        depth = -(-(parts - lag) * chans // block) * block
        low = lag * chans
        near = jnp.dot(
            mixed[:, :depth], w_ref[low : low + depth], preferred_element_type=f32
        )
        if lag == 0:
            row = lax.broadcasted_iota(jnp.int32, near.shape, 0)
            col = lax.broadcasted_iota(jnp.int32, near.shape, 1)
            near = jnp.where(col >= row, near, 0.0)
        g_ref[:, lanes * lag : lanes * lag + block] = near
    total = g_ref[:8, :]
    for top in range(8, lanes, 8):
        total = total + pltpu.roll(g_ref[top : top + 8, :], length - top, 1)
    size = 8
    while size > 1:
        size //= 2
        total = total[:size] + pltpu.roll(total[size : 2 * size], length - size, 1)
    for one in range(parts):
        out_ref[one : one + 1, :] = total[:, one * lanes : (one + 1) * lanes]
    prod = sig_ref[:, :chans].astype(f32) * sig_ref[:, chans:].astype(f32)
    bias = jnp.sum(jnp.sum(prod, axis=0).T, axis=0, keepdims=True)
    rest = jnp.zeros((1, lanes - chans), f32)
    out_ref[parts : parts + 1, :] = jnp.concatenate([bias, rest], axis=1)
    out_ref[parts + 1 :, :] = jnp.zeros((out_ref.shape[0] - parts - 1, lanes), f32)


def cross(signals):
    parts, rows, _ = signals.shape
    chans = rows // 2
    return pl.pallas_call(
        cross_kernel,
        out_shape=jax.ShapeDtypeStruct((parts + 8, lanes), f32),
        in_specs=[whole],
        out_specs=whole,
        scratch_shapes=[
            pltpu.VMEM((parts * chans + block, block), bf16),
            pltpu.VMEM((lanes, parts * lanes), f32),
        ],
        compiler_params=params,
        name="cross",
    )(signals)


def halve_kernel(pair_ref, half_ref, bias_ref):
    lines = half_ref.shape[0]
    core = lax.rem(lax.axis_index("dp"), 2)
    rows = pl.ds(pl.multiple_of(core * lines, lines), lines)
    half_ref[...] = (pair_ref[0, rows] + pair_ref[1, rows]).astype(bf16)
    line = pl.ds(2 * lines, 1)
    bias_ref[...] = (pair_ref[0, line] + pair_ref[1, line]).astype(bf16)


def halve(pair, lines):
    return pl.pallas_call(
        halve_kernel,
        out_shape=[
            jax.ShapeDtypeStruct((lines, lanes), bf16),
            jax.ShapeDtypeStruct((1, lanes), bf16),
        ],
        in_specs=[whole],
        out_specs=[whole] * 2,
        compiler_params=pltpu.CompilerParams(vmem_limit_bytes=4 << 20),
        name="halve",
    )(pair)


def final_kernel(back_ref, first_ref, value_ref, grad_ref, sums_ref, bias_ref, *rest):
    outs, held, sems = rest[:5], rest[5:10], rest[10]
    parts, chans, _ = first_ref.shape
    step = parts // final_steps
    slot = slots(parts)
    copies = []
    for at in range(final_steps):
        for one in range(at * step, (at + 1) * step):
            back_vals = back_ref[slot[one], chans:]
            held[0][one] = times(back_vals, value_ref[one])
            held[1][one] = times(grad_ref[one], back_ref[slot[one], :chans])
            held[2][one] = times(back_vals, first_ref[one])
        rows = pl.ds(at * step, step)
        for which in range(3):
            copy = pltpu.make_async_copy(
                held[which].at[rows], outs[which].at[rows], sems.at[at, which]
            )
            copy.start()
            copies.append(copy)
    sums = sums_ref[...].astype(f32)
    for line in range(sums.shape[0]):
        held[3][:, line * lanes : (line + 1) * lanes] = sums[line : line + 1]
    held[4][...] = bias_ref[0, :chans].astype(f32)
    for which in (3, 4):
        copy = pltpu.make_async_copy(held[which], outs[which], sems.at[final_steps, which - 3])
        copy.start()
        copies.append(copy)
    for copy in copies:
        copy.wait()


def final(back, first, value, grad, sums, bias):
    chans = first.shape[1]
    line = (1, sums.shape[0] * lanes)
    shapes = [(first.shape, bf16)] * 3 + [(line, f32), ((chans,), f32)]
    return pl.pallas_call(
        final_kernel,
        out_shape=[jax.ShapeDtypeStruct(*shape) for shape in shapes],
        in_specs=[whole] * 6,
        out_specs=[pl.BlockSpec(memory_space=pltpu.HBM)] * 5,
        scratch_shapes=[pltpu.VMEM(*shape) for shape in shapes]
        + [pltpu.SemaphoreType.DMA((final_steps + 1, 3))],
        compiler_params=pltpu.CompilerParams(vmem_limit_bytes=8 << 20),
        name="final",
    )(back, first, value, grad, sums, bias)


def per_device(first_gate, second_gate, value_proj, grad_out, filter_taps, skip_bias):
    ways = lax.axis_size("seq")
    chans = first_gate.shape[1] // ways
    shape = (ways, chans, lanes)
    first, second, value, grad = (
        arg.reshape(shape) for arg in (first_gate, second_gate, value_proj, grad_out)
    )
    toep = toeplitz(filter_taps)
    sent = gate(first, second, value, grad)
    order = [seq_order(ways)]
    signals = lax.all_to_all(sent, "seq", 0, 0, axis_index_groups=order, tiled=True)
    results = conv(signals, toep, skip_bias.reshape(-1, lanes))
    back = lax.all_to_all(results, "seq", 0, 0, axis_index_groups=order, tiled=True)
    partial = cross(signals)
    ranks = lax.axis_size("dp")
    cores = [[at, at + 1] for at in range(0, ranks, 2)]
    chips = [list(range(core, ranks, 2)) for core in range(2)]
    pair = lax.all_gather(partial, "dp", axis_index_groups=cores)
    half, bias = halve(pair, filter_taps.shape[1] // lanes // 2)
    half, bias = lax.psum((half, bias), "dp", axis_index_groups=chips)
    sums = lax.all_gather(half, "dp", axis_index_groups=cores, tiled=True)
    outs = final(back, first, value, grad, sums, bias)
    return (*(out.reshape(first_gate.shape) for out in outs[:3]), *outs[3:])


def solution(mesh):
    return jax.shard_map(
        per_device,
        mesh=mesh,
        in_specs=(
            P("dp", None, "seq"),
            P("dp", None, "seq"),
            P("dp", None, "seq"),
            P("dp", None, "seq"),
            P("seq", None),
            P(),
        ),
        out_specs=(
            P("dp", None, "seq"),
            P("dp", None, "seq"),
            P("dp", None, "seq"),
            P("seq", None),
            P("seq"),
        ),
        check_vma=False,
    )
```
